1024 devices in a mesh: wide: 128 (over z, y_lo, core), narrow: 8 (over y_hi, x).
Axes of the slice: x: 4, y: 4 (y_hi: 2, y_lo: 2; y = y_hi * 2 + y_lo), z: 32, core: 2. Of those that a mesh axis runs over, the one named last changes fastest.
Arguments:
- tokens: bfloat16 [32768, 1024], P('wide', 'narrow'), may hold values from -6 to 6
- gate_weight: bfloat16 [1024, 14784], P('wide', 'narrow'), may hold values from -0.1875 to 0.1875
- up_weight: bfloat16 [1024, 14784], P('wide', 'narrow'), may hold values from -0.1875 to 0.1875
Outputs:
- hidden: bfloat16 [32768, 14784], P('wide', 'narrow')
The draws below stay inside these ranges and needn't reach their ends.
All inputs are finite; a program needn't handle non-finite values.
Results may differ from the reference program's by a relative error of at most 0.001.
Values may be sent and summed in bfloat16 or wider, within the bound.
A program may use at most 32 MiB of HBM per device.

```python
import math
import jax
import jax.numpy as jnp
from jax import lax

FF = 14784
K = 1024
TOKENS = 32768


def block_scale(own_key, extent, pieces, least, largest):
    level, own = 1.0, jax.random.fold_in(own_key, 6)
    for position, shards_of in pieces:
        draws = jnp.exp(jax.random.uniform(jax.random.fold_in(own, position), (shards_of,), jnp.float32, least / len(pieces), largest / len(pieces)))
        level = level * jnp.repeat(draws, extent[position] // shards_of).reshape([-1 if axis == position else 1 for axis in range(len(extent))])
    return level


def centred(stream_key, extent, deviation, most, pieces=(), dtype=jnp.bfloat16):
    result = jax.random.normal(stream_key, extent, jnp.float32) * deviation
    if len(pieces) > 0:
        result = block_scale(stream_key, extent, pieces, -0.22, 0.18) * result
    return jnp.clip(result, min=-most, max=most).astype(dtype)


def setup_inputs(seed: int = 0) -> dict:
    arg_keys = jax.random.split(jax.random.key(seed), 4)
    return {
        "tokens": centred(arg_keys[0], (TOKENS, K), 1.0, 6.0, ((0, 128), (1, 8))),
        "gate_weight": centred(arg_keys[1], (K, FF), K ** -0.5, 0.1875, ((0, 128), (1, 8))),
        "up_weight": centred(arg_keys[2], (K, FF), K ** -0.5, 0.1875, ((0, 128), (1, 8))),
    }


def reference(tokens, gate_weight, up_weight):
    block_rows = math.gcd(TOKENS, 1024)
    blocks = tokens.reshape(TOKENS // block_rows, block_rows, K)

    def project_block(rows):
        gate = jnp.dot(rows, gate_weight, preferred_element_type=jnp.float32)
        up = jnp.dot(rows, up_weight, preferred_element_type=jnp.float32)
        return (jax.nn.silu(gate) * up).astype(jnp.bfloat16)

    return lax.map(project_block, blocks).reshape(TOKENS, FF)
```

```python
import functools
import jax
import jax.numpy as jnp
from jax import lax
from jax.experimental import pallas as pl
from jax.experimental.pallas import tpu as pltpu
from jax.sharding import PartitionSpec as P

MESH = pl.DeviceIdType.MESH
QUAD = 4
XS = 4
YS = 4
LANES = 512
CHUNKS = 2
LAG = 5.0
STRIDE = 2


def tree(planes, stride):
    right, left = planes // 2, planes - planes // 2 - 1
    parent = {}
    for sign, reach in ((1, right), (-1, left)):
        for t in range(1, reach + 1):
            parent[sign * t] = sign * (t - stride if t % stride == 0 else t - 1)
    return parent


def plan(parent):
    children = {}
    for t, p in parent.items():
        children.setdefault(p, []).append(t)
    due = {0: 0.0}

    def walk(p):
        for i, t in enumerate(children.get(p, [])):
            due[t] = due[p] + 1.8 + 0.6 * abs(t - p) + 0.3 * i
            walk(t)

    for p in children:
        children[p].sort(key=lambda t: (-abs(t - p), t))
    walk(0)
    return children, due


def kernel(
    planes, tok_ref, gate_ref, up_ref, out_ref, toks, stage, quads, weights, result, tok_send, tok_recv,
    quad_send, quad_recv, item_send, item_recv, out_send, out_recv,
):
    w, n = lax.axis_index("wide"), lax.axis_index("narrow")
    z, q = w // QUAD, w % QUAD
    core, x, y_hi, y_lo = q % 2, n % XS, n // XS, q // 2
    y = y_hi * 2 + y_lo
    parent = tree(planes, STRIDE)
    children, due = plan(parent)
    steps = sorted({t - p for t, p in parent.items()})
    steps = sorted(set(steps) | {-s for s in steps})
    each = LANES // CHUNKS

    def plane_dev(dz):
        return (lax.rem(z + dz + 2 * planes, planes) * QUAD + q, n)

    def quad_dev(k):
        return (z * QUAD + (q ^ k), n)

    def y_dev(dy):
        yy = lax.rem(y + dy, YS)
        return (z * QUAD + lax.rem(yy, 2) * 2 + core, (yy // 2) * XS + x)

    def x_dev(dx):
        return (w, y_hi * XS + lax.rem(x + dx + XS, XS))

    barrier = pltpu.get_barrier_semaphore()
    peers = [plane_dev(s) for s in steps] + [quad_dev(k) for k in (1, 2, 3)]
    peers += [y_dev(d) for d in (1, 2, 3)] + [x_dev(1), x_dev(-1)]
    for peer in peers:
        pl.semaphore_signal(barrier, inc=1, device_id=peer, device_id_type=MESH)

    full = gate_ref.shape[1]
    for k in range(QUAD):
        size = min(LANES, full - k * LANES)
        both = jnp.concatenate(
            [r[:, k * LANES : k * LANES + size].astype(jnp.float32) for r in (gate_ref, up_ref)], axis=0
        )
        if size < LANES:
            both = jnp.concatenate([both, jnp.zeros((both.shape[0], LANES - size), jnp.float32)], axis=1)
        stage[k] = both.astype(jnp.bfloat16)
    toks[core, x, y] = tok_ref[...]
    quads[q] = stage[q]
    pl.semaphore_wait(barrier, len(peers))

    def quad_copy(k):
        return pltpu.make_async_remote_copy(
            stage.at[q ^ k], quads.at[q], quad_send.at[k], quad_recv.at[k], device_id=quad_dev(k), device_id_type=MESH
        )

    for k in (3, 2, 1):
        quad_copy(k).start()

    def y_copy(d):
        block = toks.at[core, x, y]
        return pltpu.make_async_remote_copy(
            block, block, tok_send.at[d - 1], tok_recv.at[d - 1], device_id=y_dev(d), device_id_type=MESH
        )

    def x_copy(i):
        from_x = lax.rem(x + (0, 0, -1, 1)[i] + XS, XS)
        block = toks.at[core, from_x]
        if i >= 2:
            block = toks.at[core, from_x, pl.ds((i - 2) * 2, 2)]
        return pltpu.make_async_remote_copy(
            block, block, tok_send.at[3 + i], tok_recv.at[3 + i], device_id=x_dev((1, -1, 1, -1)[i]), device_id_type=MESH
        )

    def core_copy():
        block = toks.at[core]
        return pltpu.make_async_remote_copy(
            block, block, tok_send.at[7], tok_recv.at[7], device_id=quad_dev(1), device_id_type=MESH
        )

    for d in (1, 2, 3):
        y_copy(d).start()

    for k in (1, 2, 3):
        quad_copy(k).wait_recv()
    rows = [quads[s].astype(jnp.float32) for s in range(QUAD)]
    half = rows[0].shape[0] // 2
    gate_rows = jnp.concatenate([r[:half] for r in rows], axis=0).astype(jnp.bfloat16)
    up_rows = jnp.concatenate([r[half:] for r in rows], axis=0).astype(jnp.bfloat16)
    for c in range(CHUNKS):
        weights[c, z] = jnp.concatenate(
            [gate_rows[:, c * each : (c + 1) * each], up_rows[:, c * each : (c + 1) * each]], axis=1
        )

    order = sorted(((due[t] + c * LAG, c, t) for t in due for c in range(CHUNKS)))
    place = {t: i for i, t in enumerate(sorted(due))}

    def item_copy(at, to, c):
        item = weights.at[c, lax.rem(z - at + 2 * planes, planes)]
        return pltpu.make_async_remote_copy(
            item, item, item_send.at[c, place[to]], item_recv.at[c, place[to]],
            device_id=plane_dev(to - at), device_id_type=MESH,
        )

    def out_copy(c, k):
        columns = pl.ds(pl.multiple_of(q * LANES + c * each, 128), each)
        return pltpu.make_async_remote_copy(
            result.at[c, k - 1], out_ref.at[:, columns], out_send.at[c, k - 1], out_recv.at[c, k - 1],
            device_id=quad_dev(k), device_id_type=MESH,
        )

    def from_peer(c, k):
        columns = pl.ds(pl.multiple_of((q ^ k) * LANES + c * each, 128), each)
        return pltpu.make_async_remote_copy(
            result.at[c, k - 1], out_ref.at[:, columns], out_send.at[c, k - 1], out_recv.at[c, k - 1],
            device_id=quad_dev(k), device_id_type=MESH,
        )

    def compute(c):
        depth = planes * weights.shape[2]
        for k in (3, 2, 1, 0):
            row = q ^ k
            r_core, r_lo = row % 2, row // 2
            left = jnp.concatenate(
                [toks[r_core, i % XS, (i // XS) * 2 + r_lo] for i in range(2 * XS)], axis=1
            )
            right = weights[c].reshape(depth, 2 * each)
            both = jnp.dot(left, right, preferred_element_type=jnp.float32)
            gate, up = both[:, :each], both[:, each:]
            hidden = (gate / (1.0 + jnp.exp(-gate)) * up).astype(jnp.bfloat16)
            if k == 0:
                out_ref[:, pl.ds(pl.multiple_of(q * LANES + c * each, 128), each)] = hidden
            else:
                result[c, k - 1] = hidden
                out_copy(c, k).start()

    left_over = [sum(1 for _, cc, t in order if cc == c and t != 0) for c in range(CHUNKS)]
    others = [(2.0, "y"), (7.0, "x"), (13.0, "core"), (17.0, "end")]
    for when, c, t in order:
        while others and when >= others[0][0]:
            token_step(others.pop(0)[1], y_copy, x_copy, core_copy)
        if t != 0:
            item_copy(parent[t], t, c).wait_recv()
            left_over[c] -= 1
        for child in children.get(t, []):
            item_copy(t, child, c).start()
        if left_over[c] == 0:
            while others:
                token_step(others.pop(0)[1], y_copy, x_copy, core_copy)
            compute(c)

    for c in range(CHUNKS):
        for k in (1, 2, 3):
            from_peer(c, k).wait_recv()
            out_copy(c, k).wait_send()
    for k in (1, 2, 3):
        quad_copy(k).wait_send()
        y_copy(k).wait_send()
    for i in range(4):
        x_copy(i).wait_send()
    core_copy().wait_send()
    for _, c, t in order:
        for child in children.get(t, []):
            item_copy(t, child, c).wait_send()


def token_step(name, y_copy, x_copy, core_copy):
    if name == "y":
        for d in (1, 2, 3):
            y_copy(d).wait_recv()
        x_copy(0).start()
        x_copy(1).start()
    elif name == "x":
        x_copy(0).wait_recv()
        x_copy(2).start()
        x_copy(1).wait_recv()
        x_copy(3).start()
    elif name == "core":
        x_copy(2).wait_recv()
        x_copy(3).wait_recv()
        core_copy().start()
    else:
        core_copy().wait_recv()


def local(planes, tokens, gate_weight, up_weight):
    rows, depth_part = tokens.shape
    each = LANES // CHUNKS
    full = gate_weight.shape[1]
    dma = pltpu.SemaphoreType.DMA
    padded = pl.pallas_call(
        functools.partial(kernel, planes),
        out_shape=jax.ShapeDtypeStruct((rows, QUAD * LANES), jnp.bfloat16),
        in_specs=[pl.BlockSpec(memory_space=pltpu.VMEM)] * 3,
        out_specs=pl.BlockSpec(memory_space=pltpu.VMEM),
        scratch_shapes=[
            pltpu.VMEM((2, XS, YS, rows, depth_part), jnp.bfloat16),
            pltpu.VMEM((QUAD, 2 * gate_weight.shape[0], LANES), jnp.bfloat16),
            pltpu.VMEM((QUAD, 2 * gate_weight.shape[0], LANES), jnp.bfloat16),
            pltpu.VMEM((CHUNKS, planes, QUAD * gate_weight.shape[0], 2 * each), jnp.bfloat16),
            pltpu.VMEM((CHUNKS, QUAD - 1, rows, each), jnp.bfloat16),
            dma((8,)),
            dma((8,)),
            dma((QUAD,)),
            dma((QUAD,)),
            dma((CHUNKS, planes)),
            dma((CHUNKS, planes)),
            dma((CHUNKS, QUAD - 1)),
            dma((CHUNKS, QUAD - 1)),
        ],
        compiler_params=pltpu.CompilerParams(collective_id=0, has_side_effects=True, vmem_limit_bytes=40 << 20),
        cost_estimate=pl.CostEstimate(flops=4 * rows * 1024 * full, bytes_accessed=1 << 23, transcendentals=rows * full),
    )(tokens, gate_weight, up_weight)
    return padded[:, :full]


def solution(mesh):
    spec = P("wide", "narrow")
    planes = mesh.shape["wide"] // QUAD
    return jax.shard_map(
        functools.partial(local, planes), mesh=mesh, in_specs=(spec, spec, spec), out_specs=spec, check_vma=False
    )
```

```python
import functools
import jax
import jax.numpy as jnp
from jax import lax
from jax.experimental import pallas as pl
from jax.experimental.pallas import tpu as pltpu
from jax.sharding import PartitionSpec as P

MESH = pl.DeviceIdType.MESH
TEAM = 8
XS = 4
YS = 4
LANES = 256
CHUNKS = 2
LAG = 0.7
STRIDE = 1
STAGE = 4.2


def tree(planes, stride):
    right, left = planes // 2, planes - planes // 2 - 1
    parent = {}
    for sign, reach in ((1, right), (-1, left)):
        for t in range(1, reach + 1):
            parent[sign * t] = sign * (t - stride if t % stride == 0 else t - 1)
    return parent


def plan(parent):
    children = {}
    for t, p in parent.items():
        children.setdefault(p, []).append(t)
    due = {0: 0.0}

    def walk(p):
        for i, t in enumerate(children.get(p, [])):
            due[t] = due[p] + STAGE * abs(t - p) + 0.1 * i
            walk(t)

    for p in children:
        children[p].sort(key=lambda t: (-abs(t - p), t))
    walk(0)
    return children, due


def kernel(
    planes, tok_hbm, gate_hbm, up_hbm, out_ref, toks, gate_ref, up_ref, stage, quads, weights, result, load_sem, tok_send, tok_recv,
    quad_send, quad_recv, item_send, item_recv, out_send, out_recv,
):
    w, n = lax.axis_index("wide"), lax.axis_index("narrow")
    z, q = w // TEAM, w % TEAM
    core, x, y_hi, y_lo, side = q % 2, n % XS, n // XS, (q // 2) % 2, q // 4
    y = y_hi * 2 + y_lo
    parent = tree(planes, STRIDE)
    children, due = plan(parent)
    steps = sorted({t - p for t, p in parent.items()})
    steps = sorted(set(steps) | {-s for s in steps})
    each = LANES // CHUNKS

    def plane_dev(dz):
        return (lax.rem(z + dz + 2 * planes, planes) * TEAM + q, n)

    def quad_dev(k):
        return (z * TEAM + (q ^ k), n)

    def y_dev(dy):
        yy = lax.rem(y + dy, YS)
        return (z * TEAM + side * 4 + lax.rem(yy, 2) * 2 + core, (yy // 2) * XS + x)

    def x_dev(dx):
        return (w, y_hi * XS + lax.rem(x + dx + XS, XS))

    barrier = pltpu.get_barrier_semaphore()
    peers = [plane_dev(s) for s in steps] + [quad_dev(k) for k in range(1, TEAM)]
    peers += [y_dev(d) for d in (1, 2, 3)] + [x_dev(1), x_dev(-1)]
    for peer in peers:
        pl.semaphore_signal(barrier, inc=1, device_id=peer, device_id_type=MESH)

    loads = [
        pltpu.make_async_copy(gate_hbm, gate_ref, load_sem.at[0]),
        pltpu.make_async_copy(up_hbm, up_ref, load_sem.at[1]),
        pltpu.make_async_copy(tok_hbm, toks.at[core, x, y, side], load_sem.at[2]),
    ]
    for load in loads:
        load.start()
    loads[0].wait()
    loads[1].wait()

    full = gate_ref.shape[1]
    for k in range(TEAM):
        size = min(LANES, full - k * LANES)
        both = jnp.concatenate(
            [r[:, k * LANES : k * LANES + size].astype(jnp.float32) for r in (gate_ref, up_ref)], axis=0
        )
        if size < LANES:
            both = jnp.concatenate([both, jnp.zeros((both.shape[0], LANES - size), jnp.float32)], axis=1)
        stage[k] = both.astype(jnp.bfloat16)
    quads[q] = stage[q]
    loads[2].wait()
    pl.semaphore_wait(barrier, len(peers))

    def side_copy():
        block = toks.at[core, x, y, side]
        return pltpu.make_async_remote_copy(
            block, block, tok_send.at[0], tok_recv.at[0], device_id=quad_dev(4), device_id_type=MESH
        )

    def quad_copy(k):
        return pltpu.make_async_remote_copy(
            stage.at[q ^ k], quads.at[q], quad_send.at[k], quad_recv.at[k], device_id=quad_dev(k), device_id_type=MESH
        )

    for k in (6, 7, 4, 5, 2, 3, 1):
        quad_copy(k).start()
    side_copy().start()

    def y_copy(d):
        block = toks.at[core, x, y]
        return pltpu.make_async_remote_copy(
            block, block, tok_send.at[d], tok_recv.at[d], device_id=y_dev(d), device_id_type=MESH
        )

    def x_copy(i):
        from_x = lax.rem(x + (0, 0, -1, 1)[i] + XS, XS)
        block = toks.at[core, from_x]
        if i >= 2:
            block = toks.at[core, from_x, pl.ds((i - 2) * 2, 2)]
        return pltpu.make_async_remote_copy(
            block, block, tok_send.at[4 + i], tok_recv.at[4 + i], device_id=x_dev((1, -1, 1, -1)[i]), device_id_type=MESH
        )

    def core_copy(i):
        block = toks.at[core, lax.rem(x + i, XS)]
        return pltpu.make_async_remote_copy(
            block, block, tok_send.at[8 + i], tok_recv.at[8 + i], device_id=quad_dev(1), device_id_type=MESH
        )

    for k in range(1, TEAM):
        quad_copy(k).wait_recv()
    rows = [quads[s].astype(jnp.float32) for s in range(TEAM)]
    half = rows[0].shape[0] // 2
    gate_rows = jnp.concatenate([r[:half] for r in rows], axis=0).astype(jnp.bfloat16)
    up_rows = jnp.concatenate([r[half:] for r in rows], axis=0).astype(jnp.bfloat16)
    for c in range(CHUNKS):
        weights[c, z] = jnp.concatenate(
            [gate_rows[:, c * each : (c + 1) * each], up_rows[:, c * each : (c + 1) * each]], axis=1
        )

    order = sorted(((due[t] + c * LAG, c, t) for t in due for c in range(CHUNKS)))
    place = {t: i for i, t in enumerate(sorted(due))}

    def item_copy(at, to, c):
        item = weights.at[c, lax.rem(z - at + 2 * planes, planes)]
        return pltpu.make_async_remote_copy(
            item, item, item_send.at[c, place[to]], item_recv.at[c, place[to]],
            device_id=plane_dev(to - at), device_id_type=MESH,
        )

    def out_copy(c, k):
        units = pl.ds(pl.multiple_of(q * LANES + c * each, 128), each)
        return pltpu.make_async_remote_copy(
            result.at[c, k], out_ref.at[units], out_send.at[c, k], out_recv.at[c, k],
            device_id=quad_dev(k), device_id_type=MESH,
        )

    def own_copy(c):
        units = pl.ds(pl.multiple_of(q * LANES + c * each, 128), each)
        return pltpu.make_async_copy(result.at[c, 0], out_ref.at[units], out_send.at[c, 0])

    def from_peer(c, k):
        units = pl.ds(pl.multiple_of((q ^ k) * LANES + c * each, 128), each)
        return pltpu.make_async_remote_copy(
            result.at[c, k], out_ref.at[units], out_send.at[c, k], out_recv.at[c, k],
            device_id=quad_dev(k), device_id_type=MESH,
        )

    def compute(c):
        depth = planes * weights.shape[2]
        right = weights[c].reshape(depth, 2 * each).T
        for k in (7, 6, 3, 2, 5, 4, 1, 0):
            row = q ^ k
            r_core, r_lo, r_side = row % 2, (row // 2) % 2, row // 4
            left = jnp.concatenate(
                [toks[r_core, i % XS, (i // XS) * 2 + r_lo, r_side] for i in range(2 * XS)], axis=1
            )
            both = lax.dot_general(right, left, (((1,), (1,)), ((), ())), preferred_element_type=jnp.float32)
            gate, up = both[:each], both[each:]
            hidden = (gate / (1.0 + jnp.exp(-gate)) * up).astype(jnp.bfloat16)
            result[c, k] = hidden
            own_copy(c).start() if k == 0 else out_copy(c, k).start()

    left_over = [sum(1 for _, cc, t in order if cc == c and t != 0) for c in range(CHUNKS)]
    others = [(2.5, "y"), (6.0, "x"), (21.0, "x2"), (27.0, "core"), (31.0, "end")]
    for when, c, t in order:
        while others and when >= others[0][0]:
            token_step(others.pop(0)[1], side_copy, y_copy, x_copy, core_copy)
        if t != 0:
            item_copy(parent[t], t, c).wait_recv()
            left_over[c] -= 1
        for child in children.get(t, []):
            item_copy(t, child, c).start()
        if left_over[c] == 0:
            while others:
                token_step(others.pop(0)[1], side_copy, y_copy, x_copy, core_copy)
            compute(c)

    for k in range(1, TEAM):
        quad_copy(k).wait_send()
    side_copy().wait_send()
    for d in (1, 2, 3):
        y_copy(d).wait_send()
    for i in range(4):
        x_copy(i).wait_send()
        core_copy(i).wait_send()
    for _, c, t in order:
        for child in children.get(t, []):
            item_copy(t, child, c).wait_send()
    for c in range(CHUNKS):
        for k in range(1, TEAM):
            from_peer(c, k).wait_recv()
            out_copy(c, k).wait_send()
        own_copy(c).wait()


def token_step(name, side_copy, y_copy, x_copy, core_copy):
    if name == "y":
        side_copy().wait_recv()
        for d in (1, 2, 3):
            y_copy(d).start()
    elif name == "x":
        for d in (1, 2, 3):
            y_copy(d).wait_recv()
        x_copy(0).start()
        x_copy(1).start()
        core_copy(0).start()
    elif name == "x2":
        x_copy(0).wait_recv()
        x_copy(2).start()
        core_copy(3).start()
        x_copy(1).wait_recv()
        x_copy(3).start()
        core_copy(1).start()
    elif name == "core":
        x_copy(2).wait_recv()
        x_copy(3).wait_recv()
        core_copy(2).start()
    else:
        for i in range(4):
            core_copy(i).wait_recv()


def local(planes, tokens, gate_weight, up_weight):
    rows, depth_part = tokens.shape
    each = LANES // CHUNKS
    full = gate_weight.shape[1]
    dma = pltpu.SemaphoreType.DMA
    padded = pl.pallas_call(
        functools.partial(kernel, planes),
        out_shape=jax.ShapeDtypeStruct((TEAM * LANES, rows), jnp.bfloat16),
        in_specs=[pl.BlockSpec(memory_space=pltpu.HBM)] * 3,
        out_specs=pl.BlockSpec(memory_space=pltpu.HBM),
        scratch_shapes=[
            pltpu.VMEM((2, XS, YS, 2, rows, depth_part), jnp.bfloat16),
            pltpu.VMEM(gate_weight.shape, jnp.bfloat16),
            pltpu.VMEM(up_weight.shape, jnp.bfloat16),
            pltpu.VMEM((TEAM, 2 * gate_weight.shape[0], LANES), jnp.bfloat16),
            pltpu.VMEM((TEAM, 2 * gate_weight.shape[0], LANES), jnp.bfloat16),
            pltpu.VMEM((CHUNKS, planes, TEAM * gate_weight.shape[0], 2 * each), jnp.bfloat16),
            pltpu.VMEM((CHUNKS, TEAM, each, rows), jnp.bfloat16),
            dma((3,)),
            dma((12,)),
            dma((12,)),
            dma((TEAM,)),
            dma((TEAM,)),
            dma((CHUNKS, planes)),
            dma((CHUNKS, planes)),
            dma((CHUNKS, TEAM)),
            dma((CHUNKS, TEAM)),
        ],
        compiler_params=pltpu.CompilerParams(collective_id=0, has_side_effects=True, vmem_limit_bytes=61 << 20),
        cost_estimate=pl.CostEstimate(flops=4 * rows * 1024 * full, bytes_accessed=1 << 23, transcendentals=rows * full),
    )(tokens, gate_weight, up_weight)
    return padded[:full].T


def solution(mesh):
    spec = P("wide", "narrow")
    planes = mesh.shape["wide"] // TEAM
    return jax.shard_map(
        functools.partial(local, planes), mesh=mesh, in_specs=(spec, spec, spec), out_specs=spec, check_vma=False
    )
```

```python
import functools
import jax
import jax.numpy as jnp
from jax import lax
from jax.experimental import pallas as pl
from jax.experimental.pallas import tpu as pltpu
from jax.sharding import PartitionSpec as P

MESH = pl.DeviceIdType.MESH
TEAM = 8
XS = 4
YS = 4
UNITS = 240
LANES = 256
CHUNKS = 2
LAG = 0.7
STAGE = 4.2


def tree(planes, c):
    right = planes // 2 - c % 2
    parent = {t: t - 1 for t in range(1, right + 1)}
    parent.update({-t: 1 - t for t in range(1, planes - right)})
    return parent


def plan(parent):
    children = {}
    for t, p in parent.items():
        children.setdefault(p, []).append(t)
    due = {0: 0.0}

    def walk(p):
        for i, t in enumerate(children.get(p, [])):
            due[t] = due[p] + STAGE * abs(t - p) + 0.1 * i
            walk(t)

    for p in children:
        children[p].sort(key=lambda t: (-abs(t - p), t))
    walk(0)
    return children, due


def kernel(
    planes, tok_hbm, gate_hbm, up_hbm, out_ref, toks, gate_ref, up_ref, stage, quads, weights, result, load_sem, tok_send, tok_recv,
    quad_send, quad_recv, item_send, item_recv, out_send, out_recv,
):
    w, n = lax.axis_index("wide"), lax.axis_index("narrow")
    z, q = w // TEAM, w % TEAM
    core, x, y_hi, y_lo, side = q % 2, n % XS, n // XS, (q // 2) % 2, q // 4
    y = y_hi * 2 + y_lo
    parents = [tree(planes, c) for c in range(CHUNKS)]
    plans = [plan(parent) for parent in parents]
    each = LANES // CHUNKS

    def plane_dev(dz):
        return (lax.rem(z + dz + 2 * planes, planes) * TEAM + q, n)

    def quad_dev(k):
        return (z * TEAM + (q ^ k), n)

    def y_dev(dy):
        yy = lax.rem(y + dy, YS)
        return (z * TEAM + side * 4 + lax.rem(yy, 2) * 2 + core, (yy // 2) * XS + x)

    def x_dev(dx):
        return (w, y_hi * XS + lax.rem(x + dx + XS, XS))

    barrier = pltpu.get_barrier_semaphore()
    peers = [plane_dev(1), plane_dev(-1)] + [quad_dev(k) for k in range(1, TEAM)]
    peers += [y_dev(d) for d in (1, 2, 3)] + [x_dev(1), x_dev(-1)]
    for peer in peers:
        pl.semaphore_signal(barrier, inc=1, device_id=peer, device_id_type=MESH)

    loads = [
        pltpu.make_async_copy(gate_hbm, gate_ref, load_sem.at[0]),
        pltpu.make_async_copy(up_hbm, up_ref, load_sem.at[1]),
        pltpu.make_async_copy(tok_hbm, toks.at[core, x, y, side], load_sem.at[2]),
    ]
    for load in loads:
        load.start()
    loads[0].wait()
    loads[1].wait()

    full = gate_ref.shape[1]
    for k in range(TEAM):
        size = min(UNITS, full - k * UNITS)
        both = jnp.concatenate(
            [r[:, k * UNITS : k * UNITS + size].astype(jnp.float32) for r in (gate_ref, up_ref)], axis=0
        )
        if size < LANES:
            both = jnp.concatenate([both, jnp.zeros((both.shape[0], LANES - size), jnp.float32)], axis=1)
        stage[k] = both.astype(jnp.bfloat16)
    quads[q] = stage[q]
    loads[2].wait()
    pl.semaphore_wait(barrier, len(peers))

    def side_copy():
        block = toks.at[core, x, y, side]
        return pltpu.make_async_remote_copy(
            block, block, tok_send.at[0], tok_recv.at[0], device_id=quad_dev(4), device_id_type=MESH
        )

    def quad_copy(k):
        return pltpu.make_async_remote_copy(
            stage.at[q ^ k], quads.at[q], quad_send.at[k], quad_recv.at[k], device_id=quad_dev(k), device_id_type=MESH
        )

    for k in (6, 7, 4, 5, 2, 3, 1):
        quad_copy(k).start()
    side_copy().start()

    def y_copy(d):
        block = toks.at[core, x, y]
        return pltpu.make_async_remote_copy(
            block, block, tok_send.at[d], tok_recv.at[d], device_id=y_dev(d), device_id_type=MESH
        )

    def x_copy(i):
        from_x = lax.rem(x + (0, 0, -1, 1)[i] + XS, XS)
        block = toks.at[core, from_x]
        if i >= 2:
            block = toks.at[core, from_x, pl.ds((i - 2) * 2, 2)]
        return pltpu.make_async_remote_copy(
            block, block, tok_send.at[4 + i], tok_recv.at[4 + i], device_id=x_dev((1, -1, 1, -1)[i]), device_id_type=MESH
        )

    def core_copy(i):
        block = toks.at[core, lax.rem(x + i, XS)]
        return pltpu.make_async_remote_copy(
            block, block, tok_send.at[8 + i], tok_recv.at[8 + i], device_id=quad_dev(1), device_id_type=MESH
        )

    for k in range(1, TEAM):
        quad_copy(k).wait_recv()
    rows = [quads[s].astype(jnp.float32) for s in range(TEAM)]
    half = rows[0].shape[0] // 2
    gate_rows = jnp.concatenate([r[:half] for r in rows], axis=0).astype(jnp.bfloat16)
    up_rows = jnp.concatenate([r[half:] for r in rows], axis=0).astype(jnp.bfloat16)
    for c in range(CHUNKS):
        weights[c, z] = jnp.concatenate(
            [gate_rows[:, c * each : (c + 1) * each], up_rows[:, c * each : (c + 1) * each]], axis=1
        )

    order = sorted((due + c * LAG, c, t) for c in range(CHUNKS) for t, due in plans[c][1].items())
    place = {t: t + planes // 2 for t in range(-planes // 2, planes // 2 + 1)}

    def item_copy(at, to, c):
        item = weights.at[c, lax.rem(z - at + 2 * planes, planes)]
        return pltpu.make_async_remote_copy(
            item, item, item_send.at[c, place[to]], item_recv.at[c, place[to]],
            device_id=plane_dev(to - at), device_id_type=MESH,
        )

    def made(c):
        return min(each, UNITS - c * each)

    def out_copy(c, k):
        units = pl.ds(pl.multiple_of(q * UNITS + c * each, 16), made(c))
        return pltpu.make_async_remote_copy(
            result.at[c, k, pl.ds(0, made(c))], out_ref.at[units], out_send.at[c, k], out_recv.at[c, k],
            device_id=quad_dev(k), device_id_type=MESH,
        )

    def own_copy(c):
        units = pl.ds(pl.multiple_of(q * UNITS + c * each, 16), made(c))
        return pltpu.make_async_copy(result.at[c, 0, pl.ds(0, made(c))], out_ref.at[units], out_send.at[c, 0])

    def from_peer(c, k):
        units = pl.ds(pl.multiple_of((q ^ k) * UNITS + c * each, 16), made(c))
        return pltpu.make_async_remote_copy(
            result.at[c, k, pl.ds(0, made(c))], out_ref.at[units], out_send.at[c, k], out_recv.at[c, k],
            device_id=quad_dev(k), device_id_type=MESH,
        )

    def compute(c):
        depth = planes * weights.shape[2]
        right = weights[c].reshape(depth, 2 * each).T
        for k in (7, 6, 3, 2, 5, 4, 1, 0):
            row = q ^ k
            r_core, r_lo, r_side = row % 2, (row // 2) % 2, row // 4
            left = jnp.concatenate(
                [toks[r_core, i % XS, (i // XS) * 2 + r_lo, r_side] for i in range(2 * XS)], axis=1
            )
            both = lax.dot_general(right, left, (((1,), (1,)), ((), ())), preferred_element_type=jnp.float32)
            gate, up = both[:each], both[each:]
            hidden = (gate / (1.0 + jnp.exp(-gate)) * up).astype(jnp.bfloat16)
            result[c, k] = hidden
            own_copy(c).start() if k == 0 else out_copy(c, k).start()

    left_over = [sum(1 for _, cc, t in order if cc == c and t != 0) for c in range(CHUNKS)]
    others = [(2.5, "y"), (6.0, "x"), (21.0, "x2"), (27.0, "core"), (31.0, "end")]
    for when, c, t in order:
        while others and when >= others[0][0]:
            token_step(others.pop(0)[1], side_copy, y_copy, x_copy, core_copy)
        if t != 0:
            item_copy(parents[c][t], t, c).wait_recv()
            left_over[c] -= 1
        for child in plans[c][0].get(t, []):
            item_copy(t, child, c).start()
        if left_over[c] == 0:
            while others:
                token_step(others.pop(0)[1], side_copy, y_copy, x_copy, core_copy)
            compute(c)

    for k in range(1, TEAM):
        quad_copy(k).wait_send()
    side_copy().wait_send()
    for d in (1, 2, 3):
        y_copy(d).wait_send()
    for i in range(4):
        x_copy(i).wait_send()
        core_copy(i).wait_send()
    for _, c, t in order:
        for child in plans[c][0].get(t, []):
            item_copy(t, child, c).wait_send()
    for c in range(CHUNKS):
        for k in range(1, TEAM):
            from_peer(c, k).wait_recv()
            out_copy(c, k).wait_send()
        own_copy(c).wait()


def token_step(name, side_copy, y_copy, x_copy, core_copy):
    if name == "y":
        side_copy().wait_recv()
        for d in (1, 2, 3):
            y_copy(d).start()
    elif name == "x":
        for d in (1, 2, 3):
            y_copy(d).wait_recv()
        x_copy(0).start()
        x_copy(1).start()
        core_copy(0).start()
    elif name == "x2":
        x_copy(0).wait_recv()
        x_copy(2).start()
        core_copy(3).start()
        x_copy(1).wait_recv()
        x_copy(3).start()
        core_copy(1).start()
    elif name == "core":
        x_copy(2).wait_recv()
        x_copy(3).wait_recv()
        core_copy(2).start()
    else:
        for i in range(4):
            core_copy(i).wait_recv()


def local(planes, tokens, gate_weight, up_weight):
    rows, depth_part = tokens.shape
    each = LANES // CHUNKS
    full = gate_weight.shape[1]
    dma = pltpu.SemaphoreType.DMA
    padded = pl.pallas_call(
        functools.partial(kernel, planes),
        out_shape=jax.ShapeDtypeStruct((TEAM * UNITS, rows), jnp.bfloat16),
        in_specs=[pl.BlockSpec(memory_space=pltpu.HBM)] * 3,
        out_specs=pl.BlockSpec(memory_space=pltpu.HBM),
        scratch_shapes=[
            pltpu.VMEM((2, XS, YS, 2, rows, depth_part), jnp.bfloat16),
            pltpu.VMEM(gate_weight.shape, jnp.bfloat16),
            pltpu.VMEM(up_weight.shape, jnp.bfloat16),
            pltpu.VMEM((TEAM, 2 * gate_weight.shape[0], LANES), jnp.bfloat16),
            pltpu.VMEM((TEAM, 2 * gate_weight.shape[0], LANES), jnp.bfloat16),
            pltpu.VMEM((CHUNKS, planes, TEAM * gate_weight.shape[0], 2 * each), jnp.bfloat16),
            pltpu.VMEM((CHUNKS, TEAM, each, rows), jnp.bfloat16),
            dma((3,)),
            dma((12,)),
            dma((12,)),
            dma((TEAM,)),
            dma((TEAM,)),
            dma((CHUNKS, planes + 1)),
            dma((CHUNKS, planes + 1)),
            dma((CHUNKS, TEAM)),
            dma((CHUNKS, TEAM)),
        ],
        compiler_params=pltpu.CompilerParams(collective_id=0, has_side_effects=True, vmem_limit_bytes=61 << 20),
        cost_estimate=pl.CostEstimate(flops=4 * rows * 1024 * full, bytes_accessed=1 << 23, transcendentals=rows * full),
    )(tokens, gate_weight, up_weight)
    return padded[:full].T


def solution(mesh):
    spec = P("wide", "narrow")
    planes = mesh.shape["wide"] // TEAM
    return jax.shard_map(
        functools.partial(local, planes), mesh=mesh, in_specs=(spec, spec, spec), out_specs=spec, check_vma=False
    )
```

```python
import functools
import jax
import jax.numpy as jnp
from jax import lax
from jax.experimental import pallas as pl
from jax.experimental.pallas import tpu as pltpu
from jax.sharding import PartitionSpec as P

MESH = pl.DeviceIdType.MESH
TEAM = 8
XS = 4
YS = 4
UNITS = 240
LANES = 256
CHUNKS = 2
LAG = 0.7
STAGE = 4.2


def tree(planes, c):
    right = planes // 2 - c % 2
    parent = {t: t - 1 for t in range(1, right + 1)}
    parent.update({-t: 1 - t for t in range(1, planes - right)})
    return parent


def plan(parent):
    children = {}
    for t, p in parent.items():
        children.setdefault(p, []).append(t)
    due = {0: 0.0}

    def walk(p):
        for i, t in enumerate(children.get(p, [])):
            due[t] = due[p] + STAGE * abs(t - p) + 0.1 * i
            walk(t)

    for p in children:
        children[p].sort(key=lambda t: (-abs(t - p), t))
    walk(0)
    return children, due


def kernel(
    planes, tok_hbm, gate_hbm, up_hbm, out_ref, toks, gate_ref, up_ref, stage, quads, weights, result, load_sem, tok_send, tok_recv,
    quad_send, quad_recv, item_send, item_recv, out_send, out_recv,
):
    w, n = lax.axis_index("wide"), lax.axis_index("narrow")
    z, q = w // TEAM, w % TEAM
    core, x, y_hi, y_lo, side = q % 2, n % XS, n // XS, (q // 2) % 2, q // 4
    y = y_hi * 2 + y_lo
    parents = [tree(planes, c) for c in range(CHUNKS)]
    plans = [plan(parent) for parent in parents]
    each = LANES // CHUNKS

    def plane_dev(dz):
        return (lax.rem(z + dz + 2 * planes, planes) * TEAM + q, n)

    def quad_dev(k):
        return (z * TEAM + (q ^ k), n)

    def y_dev(dy):
        yy = lax.rem(y + dy, YS)
        return (z * TEAM + side * 4 + lax.rem(yy, 2) * 2 + core, (yy // 2) * XS + x)

    def x_dev(dx):
        return (w, y_hi * XS + lax.rem(x + dx + XS, XS))

    loads = [
        pltpu.make_async_copy(gate_hbm, gate_ref, load_sem.at[0]),
        pltpu.make_async_copy(up_hbm, up_ref, load_sem.at[1]),
        pltpu.make_async_copy(tok_hbm, toks.at[core, x, y, side], load_sem.at[2]),
    ]
    for load in loads:
        load.start()
    barrier = pltpu.get_barrier_semaphore()
    peers = [plane_dev(1), plane_dev(-1)] + [quad_dev(k) for k in range(1, TEAM)]
    peers += [y_dev(d) for d in (1, 2, 3)] + [x_dev(1), x_dev(-1)]
    for peer in peers:
        pl.semaphore_signal(barrier, inc=1, device_id=peer, device_id_type=MESH)

    loads[0].wait()
    loads[1].wait()

    full = gate_ref.shape[1]
    for k in range(TEAM):
        size = min(UNITS, full - k * UNITS)
        both = jnp.concatenate(
            [r[:, k * UNITS : k * UNITS + size].astype(jnp.float32) for r in (gate_ref, up_ref)], axis=0
        )
        if size < LANES:
            both = jnp.concatenate([both, jnp.zeros((both.shape[0], LANES - size), jnp.float32)], axis=1)
        stage[k] = both.astype(jnp.bfloat16)
    quads[q] = stage[q]
    loads[2].wait()
    pl.semaphore_wait(barrier, len(peers))

    def side_copy():
        block = toks.at[core, x, y, side]
        return pltpu.make_async_remote_copy(
            block, block, tok_send.at[0], tok_recv.at[0], device_id=quad_dev(4), device_id_type=MESH
        )

    def quad_copy(k):
        return pltpu.make_async_remote_copy(
            stage.at[q ^ k], quads.at[q], quad_send.at[k], quad_recv.at[k], device_id=quad_dev(k), device_id_type=MESH
        )

    for k in (6, 7, 4, 5, 2, 3, 1):
        quad_copy(k).start()
    side_copy().start()

    def y_copy(d):
        block = toks.at[core, x, y]
        return pltpu.make_async_remote_copy(
            block, block, tok_send.at[d], tok_recv.at[d], device_id=y_dev(d), device_id_type=MESH
        )

    def x_copy(i):
        from_x = lax.rem(x + (0, 0, -1, 1)[i] + XS, XS)
        block = toks.at[core, from_x]
        if i >= 2:
            block = toks.at[core, from_x, pl.ds((i - 2) * 2, 2)]
        return pltpu.make_async_remote_copy(
            block, block, tok_send.at[4 + i], tok_recv.at[4 + i], device_id=x_dev((1, -1, 1, -1)[i]), device_id_type=MESH
        )

    def core_copy(i):
        block = toks.at[core, lax.rem(x + i, XS)]
        return pltpu.make_async_remote_copy(
            block, block, tok_send.at[8 + i], tok_recv.at[8 + i], device_id=quad_dev(1), device_id_type=MESH
        )

    for k in range(1, TEAM):
        quad_copy(k).wait_recv()
    rows = [quads[s].astype(jnp.float32) for s in range(TEAM)]
    half = rows[0].shape[0] // 2
    gate_rows = jnp.concatenate([r[:half] for r in rows], axis=0).astype(jnp.bfloat16)
    up_rows = jnp.concatenate([r[half:] for r in rows], axis=0).astype(jnp.bfloat16)
    for c in range(CHUNKS):
        weights[c, z] = jnp.concatenate(
            [gate_rows[:, c * each : (c + 1) * each], up_rows[:, c * each : (c + 1) * each]], axis=1
        )

    order = sorted((due + c * LAG, c, t) for c in range(CHUNKS) for t, due in plans[c][1].items())
    place = {t: t + planes // 2 for t in range(-planes // 2, planes // 2 + 1)}

    def item_copy(at, to, c):
        item = weights.at[c, lax.rem(z - at + 2 * planes, planes)]
        return pltpu.make_async_remote_copy(
            item, item, item_send.at[c, place[to]], item_recv.at[c, place[to]],
            device_id=plane_dev(to - at), device_id_type=MESH,
        )

    def made(c):
        return min(each, UNITS - c * each)

    def out_copy(c, k):
        units = pl.ds(pl.multiple_of(q * UNITS + c * each, 16), made(c))
        return pltpu.make_async_remote_copy(
            result.at[c, k, pl.ds(0, made(c))], out_ref.at[units], out_send.at[c, k], out_recv.at[c, k],
            device_id=quad_dev(k), device_id_type=MESH,
        )

    def own_copy(c):
        units = pl.ds(pl.multiple_of(q * UNITS + c * each, 16), made(c))
        return pltpu.make_async_copy(result.at[c, 0, pl.ds(0, made(c))], out_ref.at[units], out_send.at[c, 0])

    def from_peer(c, k):
        units = pl.ds(pl.multiple_of((q ^ k) * UNITS + c * each, 16), made(c))
        return pltpu.make_async_remote_copy(
            result.at[c, k, pl.ds(0, made(c))], out_ref.at[units], out_send.at[c, k], out_recv.at[c, k],
            device_id=quad_dev(k), device_id_type=MESH,
        )

    def compute(c):
        depth = planes * weights.shape[2]
        right = weights[c].reshape(depth, 2 * each).T
        for k in (7, 3, 5, 6, 2, 4, 1, 0):
            row = q ^ k
            r_core, r_lo, r_side = row % 2, (row // 2) % 2, row // 4
            left = jnp.concatenate(
                [toks[r_core, i % XS, (i // XS) * 2 + r_lo, r_side] for i in range(2 * XS)], axis=1
            )
            both = lax.dot_general(right, left, (((1,), (1,)), ((), ())), preferred_element_type=jnp.float32)
            gate, up = both[:each], both[each:]
            hidden = (gate / (1.0 + jnp.exp(-gate)) * up).astype(jnp.bfloat16)
            result[c, k] = hidden
            own_copy(c).start() if k == 0 else out_copy(c, k).start()

    left_over = [sum(1 for _, cc, t in order if cc == c and t != 0) for c in range(CHUNKS)]
    others = [(2.5, "y"), (6.0, "x"), (21.0, "x2"), (27.0, "core"), (31.0, "end")]
    for when, c, t in order:
        while others and when >= others[0][0]:
            token_step(others.pop(0)[1], side_copy, y_copy, x_copy, core_copy)
        if t != 0:
            item_copy(parents[c][t], t, c).wait_recv()
            left_over[c] -= 1
        for child in plans[c][0].get(t, []):
            item_copy(t, child, c).start()
        if left_over[c] == 0:
            while others:
                token_step(others.pop(0)[1], side_copy, y_copy, x_copy, core_copy)
            compute(c)

    for k in range(1, TEAM):
        quad_copy(k).wait_send()
    side_copy().wait_send()
    for d in (1, 2, 3):
        y_copy(d).wait_send()
    for i in range(4):
        x_copy(i).wait_send()
        core_copy(i).wait_send()
    for _, c, t in order:
        for child in plans[c][0].get(t, []):
            item_copy(t, child, c).wait_send()
    for c in range(CHUNKS):
        for k in range(1, TEAM):
            from_peer(c, k).wait_recv()
            out_copy(c, k).wait_send()
        own_copy(c).wait()


def token_step(name, side_copy, y_copy, x_copy, core_copy):
    if name == "y":
        side_copy().wait_recv()
        for d in (1, 2, 3):
            y_copy(d).start()
    elif name == "x":
        for d in (1, 2, 3):
            y_copy(d).wait_recv()
        x_copy(0).start()
        x_copy(1).start()
        core_copy(0).start()
    elif name == "x2":
        x_copy(0).wait_recv()
        x_copy(2).start()
        core_copy(3).start()
        x_copy(1).wait_recv()
        x_copy(3).start()
        core_copy(1).start()
    elif name == "core":
        x_copy(2).wait_recv()
        x_copy(3).wait_recv()
        core_copy(2).start()
    else:
        for i in range(4):
            core_copy(i).wait_recv()


def local(planes, tokens, gate_weight, up_weight):
    rows, depth_part = tokens.shape
    each = LANES // CHUNKS
    full = gate_weight.shape[1]
    dma = pltpu.SemaphoreType.DMA
    padded = pl.pallas_call(
        functools.partial(kernel, planes),
        out_shape=jax.ShapeDtypeStruct((TEAM * UNITS, rows), jnp.bfloat16),
        in_specs=[pl.BlockSpec(memory_space=pltpu.HBM)] * 3,
        out_specs=pl.BlockSpec(memory_space=pltpu.HBM),
        scratch_shapes=[
            pltpu.VMEM((2, XS, YS, 2, rows, depth_part), jnp.bfloat16),
            pltpu.VMEM(gate_weight.shape, jnp.bfloat16),
            pltpu.VMEM(up_weight.shape, jnp.bfloat16),
            pltpu.VMEM((TEAM, 2 * gate_weight.shape[0], LANES), jnp.bfloat16),
            pltpu.VMEM((TEAM, 2 * gate_weight.shape[0], LANES), jnp.bfloat16),
            pltpu.VMEM((CHUNKS, planes, TEAM * gate_weight.shape[0], 2 * each), jnp.bfloat16),
            pltpu.VMEM((CHUNKS, TEAM, each, rows), jnp.bfloat16),
            dma((3,)),
            dma((12,)),
            dma((12,)),
            dma((TEAM,)),
            dma((TEAM,)),
            dma((CHUNKS, planes + 1)),
            dma((CHUNKS, planes + 1)),
            dma((CHUNKS, TEAM)),
            dma((CHUNKS, TEAM)),
        ],
        compiler_params=pltpu.CompilerParams(collective_id=0, has_side_effects=True, vmem_limit_bytes=61 << 20),
        cost_estimate=pl.CostEstimate(flops=4 * rows * 1024 * full, bytes_accessed=1 << 23, transcendentals=rows * full),
    )(tokens, gate_weight, up_weight)
    return padded[:full].T


def solution(mesh):
    spec = P("wide", "narrow")
    planes = mesh.shape["wide"] // TEAM
    return jax.shard_map(
        functools.partial(local, planes), mesh=mesh, in_specs=(spec, spec, spec), out_specs=spec, check_vma=False
    )
```

```python
import functools
import jax
import jax.numpy as jnp
from jax import lax
from jax.experimental import pallas as pl
from jax.experimental.pallas import tpu as pltpu
from jax.sharding import PartitionSpec as P

MESH = pl.DeviceIdType.MESH
TEAM = 8
XS = 4
YS = 4
UNITS = 240
LANES = 256
CHUNKS = 2
LAG = 0.7
STAGE = 4.2


def tree(planes, c):
    right = planes // 2 - c % 2
    parent = {t: t - 1 for t in range(1, right + 1)}
    parent.update({-t: 1 - t for t in range(1, planes - right)})
    return parent


def plan(parent):
    children = {}
    for t, p in parent.items():
        children.setdefault(p, []).append(t)
    due = {0: 0.0}

    def walk(p):
        for i, t in enumerate(children.get(p, [])):
            due[t] = due[p] + STAGE * abs(t - p) + 0.1 * i
            walk(t)

    for p in children:
        children[p].sort(key=lambda t: (-abs(t - p), t))
    walk(0)
    return children, due


def kernel(
    planes, tok_hbm, gate_hbm, up_hbm, out_ref, toks, gate_ref, up_ref, stage, quads, weights, result, load_sem, tok_send, tok_recv,
    quad_send, quad_recv, item_send, item_recv, out_send, out_recv,
):
    w, n = lax.axis_index("wide"), lax.axis_index("narrow")
    z, q = w // TEAM, w % TEAM
    core, x, y_hi, y_lo, side = q % 2, n % XS, n // XS, (q // 2) % 2, q // 4
    y = y_hi * 2 + y_lo
    parents = [tree(planes, c) for c in range(CHUNKS)]
    plans = [plan(parent) for parent in parents]
    each = LANES // CHUNKS

    def plane_dev(dz):
        return (lax.rem(z + dz + 2 * planes, planes) * TEAM + q, n)

    def quad_dev(k):
        return (z * TEAM + (q ^ k), n)

    def y_dev(dy):
        yy = y ^ dy
        return (z * TEAM + side * 4 + lax.rem(yy, 2) * 2 + core, (yy // 2) * XS + x)

    def x_dev(dx):
        return (w, y_hi * XS + lax.rem(x + dx + XS, XS))

    loads = [
        pltpu.make_async_copy(gate_hbm, gate_ref, load_sem.at[0]),
        pltpu.make_async_copy(up_hbm, up_ref, load_sem.at[1]),
        pltpu.make_async_copy(tok_hbm, toks.at[core, x, y, side], load_sem.at[2]),
    ]
    for load in loads:
        load.start()
    barrier = pltpu.get_barrier_semaphore()
    peers = [plane_dev(1), plane_dev(-1)] + [quad_dev(k) for k in range(1, TEAM)]
    peers += [y_dev(2), y_dev(3)] + [x_dev(1), x_dev(-1)]
    for peer in peers:
        pl.semaphore_signal(barrier, inc=1, device_id=peer, device_id_type=MESH)

    loads[0].wait()
    loads[1].wait()

    full = gate_ref.shape[1]
    for k in range(TEAM):
        size = min(UNITS, full - k * UNITS)
        both = jnp.concatenate(
            [r[:, k * UNITS : k * UNITS + size].astype(jnp.float32) for r in (gate_ref, up_ref)], axis=0
        )
        if size < LANES:
            both = jnp.concatenate([both, jnp.zeros((both.shape[0], LANES - size), jnp.float32)], axis=1)
        stage[k] = both.astype(jnp.bfloat16)
    quads[q] = stage[q]
    loads[2].wait()
    pl.semaphore_wait(barrier, len(peers))

    def side_copy():
        block = toks.at[core, x, y, side]
        return pltpu.make_async_remote_copy(
            block, block, tok_send.at[0], tok_recv.at[0], device_id=quad_dev(4), device_id_type=MESH
        )

    def quad_copy(k):
        return pltpu.make_async_remote_copy(
            stage.at[q ^ k], quads.at[q], quad_send.at[k], quad_recv.at[k], device_id=quad_dev(k), device_id_type=MESH
        )

    for k in (6, 7, 4, 5, 2, 3, 1):
        quad_copy(k).start()
    side_copy().start()

    def y_copy(d):
        block = toks.at[core, x, y]
        return pltpu.make_async_remote_copy(
            block, block, tok_send.at[d], tok_recv.at[d], device_id=y_dev(d), device_id_type=MESH
        )

    def x_copy(i):
        from_x = lax.rem(x + (0, 0, -1, 1)[i] + XS, XS)
        block = toks.at[core, from_x]
        if i >= 2:
            block = toks.at[core, from_x, pl.ds((i - 2) * 2, 2)]
        return pltpu.make_async_remote_copy(
            block, block, tok_send.at[4 + i], tok_recv.at[4 + i], device_id=x_dev((1, -1, 1, -1)[i]), device_id_type=MESH
        )

    def core_copy(i):
        block = toks.at[core, lax.rem(x + i, XS)]
        return pltpu.make_async_remote_copy(
            block, block, tok_send.at[8 + i], tok_recv.at[8 + i], device_id=quad_dev(1), device_id_type=MESH
        )

    for k in range(1, TEAM):
        quad_copy(k).wait_recv()
    rows = [quads[s].astype(jnp.float32) for s in range(TEAM)]
    half = rows[0].shape[0] // 2
    gate_rows = jnp.concatenate([r[:half] for r in rows], axis=0).astype(jnp.bfloat16)
    up_rows = jnp.concatenate([r[half:] for r in rows], axis=0).astype(jnp.bfloat16)
    for c in range(CHUNKS):
        weights[c, z] = jnp.concatenate(
            [gate_rows[:, c * each : (c + 1) * each], up_rows[:, c * each : (c + 1) * each]], axis=1
        )

    order = sorted((due + c * LAG, c, t) for c in range(CHUNKS) for t, due in plans[c][1].items())
    place = {t: t + planes // 2 for t in range(-planes // 2, planes // 2 + 1)}

    def item_copy(at, to, c):
        item = weights.at[c, lax.rem(z - at + 2 * planes, planes)]
        return pltpu.make_async_remote_copy(
            item, item, item_send.at[c, place[to]], item_recv.at[c, place[to]],
            device_id=plane_dev(to - at), device_id_type=MESH,
        )

    def made(c):
        return min(each, UNITS - c * each)

    def out_copy(c, k):
        units = pl.ds(pl.multiple_of(q * UNITS + c * each, 16), made(c))
        return pltpu.make_async_remote_copy(
            result.at[c, k, pl.ds(0, made(c))], out_ref.at[units], out_send.at[c, k], out_recv.at[c, k],
            device_id=quad_dev(k), device_id_type=MESH,
        )

    def own_copy(c):
        units = pl.ds(pl.multiple_of(q * UNITS + c * each, 16), made(c))
        return pltpu.make_async_copy(result.at[c, 0, pl.ds(0, made(c))], out_ref.at[units], out_send.at[c, 0])

    def from_peer(c, k):
        units = pl.ds(pl.multiple_of((q ^ k) * UNITS + c * each, 16), made(c))
        return pltpu.make_async_remote_copy(
            result.at[c, k, pl.ds(0, made(c))], out_ref.at[units], out_send.at[c, k], out_recv.at[c, k],
            device_id=quad_dev(k), device_id_type=MESH,
        )

    def compute(c):
        depth = planes * weights.shape[2]
        right = weights[c].reshape(depth, 2 * each).T
        for k in (7, 3, 5, 6, 2, 4, 1, 0):
            row = q ^ k
            r_core, r_lo, r_side = row % 2, (row // 2) % 2, row // 4
            left = jnp.concatenate(
                [toks[r_core, i % XS, (i // XS) * 2 + r_lo, r_side] for i in range(2 * XS)], axis=1
            )
            both = lax.dot_general(right, left, (((1,), (1,)), ((), ())), preferred_element_type=jnp.float32)
            gate, up = both[:each], both[each:]
            hidden = (gate / (1.0 + jnp.exp(-gate)) * up).astype(jnp.bfloat16)
            result[c, k] = hidden
            own_copy(c).start() if k == 0 else out_copy(c, k).start()

    left_over = [sum(1 for _, cc, t in order if cc == c and t != 0) for c in range(CHUNKS)]
    others = [(2.5, "y"), (6.0, "x"), (21.0, "x2"), (27.0, "core"), (31.0, "end")]
    for when, c, t in order:
        while others and when >= others[0][0]:
            token_step(others.pop(0)[1], side_copy, y_copy, x_copy, core_copy)
        if t != 0:
            item_copy(parents[c][t], t, c).wait_recv()
            left_over[c] -= 1
        for child in plans[c][0].get(t, []):
            item_copy(t, child, c).start()
        if left_over[c] == 0:
            while others:
                token_step(others.pop(0)[1], side_copy, y_copy, x_copy, core_copy)
            compute(c)

    for k in range(1, TEAM):
        quad_copy(k).wait_send()
    side_copy().wait_send()
    for d in (1, 2, 3):
        y_copy(d).wait_send()
    for i in range(4):
        x_copy(i).wait_send()
        core_copy(i).wait_send()
    for _, c, t in order:
        for child in plans[c][0].get(t, []):
            item_copy(t, child, c).wait_send()
    for c in range(CHUNKS):
        for k in range(1, TEAM):
            from_peer(c, k).wait_recv()
            out_copy(c, k).wait_send()
        own_copy(c).wait()


def token_step(name, side_copy, y_copy, x_copy, core_copy):
    if name == "y":
        side_copy().wait_recv()
        for d in (1, 2, 3):
            y_copy(d).start()
    elif name == "x":
        for d in (1, 2, 3):
            y_copy(d).wait_recv()
        x_copy(0).start()
        x_copy(1).start()
        core_copy(0).start()
    elif name == "x2":
        x_copy(0).wait_recv()
        x_copy(2).start()
        core_copy(3).start()
        x_copy(1).wait_recv()
        x_copy(3).start()
        core_copy(1).start()
    elif name == "core":
        x_copy(2).wait_recv()
        x_copy(3).wait_recv()
        core_copy(2).start()
    else:
        for i in range(4):
            core_copy(i).wait_recv()


def local(planes, tokens, gate_weight, up_weight):
    rows, depth_part = tokens.shape
    each = LANES // CHUNKS
    full = gate_weight.shape[1]
    dma = pltpu.SemaphoreType.DMA
    padded = pl.pallas_call(
        functools.partial(kernel, planes),
        out_shape=jax.ShapeDtypeStruct((TEAM * UNITS, rows), jnp.bfloat16),
        in_specs=[pl.BlockSpec(memory_space=pltpu.HBM)] * 3,
        out_specs=pl.BlockSpec(memory_space=pltpu.HBM),
        scratch_shapes=[
            pltpu.VMEM((2, XS, YS, 2, rows, depth_part), jnp.bfloat16),
            pltpu.VMEM(gate_weight.shape, jnp.bfloat16),
            pltpu.VMEM(up_weight.shape, jnp.bfloat16),
            pltpu.VMEM((TEAM, 2 * gate_weight.shape[0], LANES), jnp.bfloat16),
            pltpu.VMEM((TEAM, 2 * gate_weight.shape[0], LANES), jnp.bfloat16),
            pltpu.VMEM((CHUNKS, planes, TEAM * gate_weight.shape[0], 2 * each), jnp.bfloat16),
            pltpu.VMEM((CHUNKS, TEAM, each, rows), jnp.bfloat16),
            dma((3,)),
            dma((12,)),
            dma((12,)),
            dma((TEAM,)),
            dma((TEAM,)),
            dma((CHUNKS, planes + 1)),
            dma((CHUNKS, planes + 1)),
            dma((CHUNKS, TEAM)),
            dma((CHUNKS, TEAM)),
        ],
        compiler_params=pltpu.CompilerParams(collective_id=0, has_side_effects=True, vmem_limit_bytes=61 << 20),
        cost_estimate=pl.CostEstimate(flops=4 * rows * 1024 * full, bytes_accessed=1 << 23, transcendentals=rows * full),
    )(tokens, gate_weight, up_weight)
    return padded[:full].T


def solution(mesh):
    spec = P("wide", "narrow")
    planes = mesh.shape["wide"] // TEAM
    return jax.shard_map(
        functools.partial(local, planes), mesh=mesh, in_specs=(spec, spec, spec), out_specs=spec, check_vma=False
    )
```
